512 devices in a mesh: tm: 16 (over x, y), rows: 32 (over z, core).
Axes of the slice: x: 4, y: 4, z: 16, core: 2. Of those that a mesh axis runs over, the one named last changes fastest.
Arguments:
- queries: bfloat16 [16, 64, 128, 1152], P('tm', 'rows'), may hold values from -6 to 6
- keys: bfloat16 [16, 64, 128, 1152], P('tm', 'rows'), may hold values from -18 to 18
- values: bfloat16 [16, 64, 128, 1152], P('tm', 'rows'), may hold values from -4.8 to 12
- cotangent: bfloat16 [16, 64, 128, 1152], P('tm', 'rows'), may hold values from -6 to 6
- kernel: float32 [3, 3, 1152], replicated, may hold values from -1.2 to 1.2
Outputs:
- grad_queries: bfloat16 [16, 64, 128, 1152], P('tm', 'rows')
- grad_keys: bfloat16 [16, 64, 128, 1152], P('tm', 'rows')
- grad_values: bfloat16 [16, 64, 128, 1152], P('tm', 'rows')
- grad_kernel: float32 [3, 3, 1152], replicated
The draws below stay inside these ranges and needn't reach their ends.
All inputs are finite; a program needn't handle non-finite values.
Results may differ from the reference program's by a relative error of at most 0.008.
Values may be sent and summed in bfloat16 or wider, within the bound.
A program may use at most 64 MiB of HBM per device.

```python
import jax
import jax.numpy as jnp
from jax import lax

HEADS = 36
HEAD_DIM = 32
COLS = 128
FRAMES = 16
ROWS = 64
TOKENS = 131072


def shared_field(key):
    shape = (FRAMES, ROWS, COLS, HEADS * HEAD_DIM)
    return jnp.clip(jax.random.normal(key, shape, jnp.float32), -6.0, 6.0)


def draw_keys(key, part):
    common = shared_field(key)
    rising = 1.0 + 2.0 * jnp.arange(FRAMES, dtype=jnp.float32) / max(FRAMES - 1, 1)
    field = common * rising[:, None, None, None]
    return jnp.clip(field, -18.0, 18.0).astype(jnp.bfloat16)


def draw_values(key, part):
    common = shared_field(key)
    key = jax.random.fold_in(key, 13)
    noise = jnp.clip(jax.random.normal(key, common.shape, jnp.float32), -6.0, 6.0)
    weight = 0.6
    return (0.8 * noise + weight * jnp.maximum(common, 0.0)).astype(jnp.bfloat16)


def block_levels(own_key, extent, split, low, largest):
    gain = 1.0
    for position, blocks in split:
        draws = jax.random.uniform(jax.random.fold_in(jax.random.fold_in(own_key, 6), position), (blocks,), jnp.float32, low / len(split), largest / len(split))
        gain = gain * jnp.repeat(jnp.exp(draws), extent[position] // blocks).reshape((-1,) + (1,) * (len(extent) - 1 - position))
    return gain


def centred(stream_key, dims, spread, limit, cuts=(), kind=jnp.bfloat16):
    gain = block_levels(stream_key, dims, cuts, -0.22, 0.18) if cuts else 1.0
    entries = jax.random.normal(stream_key, dims, jnp.float32) * spread * gain
    return jnp.minimum(jnp.maximum(entries, -limit), limit).astype(kind)


def setup_inputs(seed: int = 0) -> dict:
    splits = jax.random.split(jax.random.key(seed), 6)
    return {
        "queries": centred(splits[0], (FRAMES, ROWS, COLS, HEADS * HEAD_DIM), 1.0, 6.0, ((0, 16), (1, 32))),
        "keys": draw_keys(jax.random.fold_in(splits[5], 71), 0),
        "values": draw_values(jax.random.fold_in(splits[5], 71), 0),
        "cotangent": centred(splits[3], (FRAMES, ROWS, COLS, HEADS * HEAD_DIM), 1.0, 6.0, ((0, 16), (1, 32))),
        "kernel": centred(splits[4], (3, 3, HEADS * HEAD_DIM), 0.3, 1.2, (), jnp.float32),
    }


DEN_EPS = 0.1
HIGH = lax.Precision.HIGHEST


def head_grads(queries, keys, values, cotangent, kernel, head):
    start = head * HEAD_DIM

    def piece(x):
        return lax.dynamic_slice_in_dim(x, start, HEAD_DIM, 3)

    q_head = piece(queries)
    k_head = piece(keys)
    v_head = piece(values)
    g_head = piece(cotangent)
    ker = lax.dynamic_slice_in_dim(kernel, start, HEAD_DIM, 2)
    shape = q_head.shape
    q_flat = q_head.reshape(-1, HEAD_DIM).astype(jnp.float32)
    k_flat = k_head.reshape(-1, HEAD_DIM).astype(jnp.float32)
    v_flat = v_head.reshape(-1, HEAD_DIM).astype(jnp.float32)
    g_flat = g_head.reshape(-1, HEAD_DIM).astype(jnp.float32)
    pos_q = jnp.maximum(q_flat, 0.0)
    pos_k = jnp.maximum(k_flat, 0.0)
    states = jnp.dot(pos_k.T, v_flat, precision=HIGH) / TOKENS
    keysum = jnp.sum(pos_k, axis=0) / TOKENS
    den = jnp.dot(pos_q, keysum, precision=HIGH) + DEN_EPS
    num = jnp.dot(pos_q, states, precision=HIGH)
    dnum = g_flat / den[:, None]
    dden = -jnp.sum(g_flat * num, axis=1) / (den * den)
    dpos_q = jnp.dot(dnum, states.T, precision=HIGH) + dden[:, None] * keysum[None, :]
    grad_q = jnp.where(q_flat > 0, dpos_q, 0.0)
    gstate = jnp.dot(pos_q.T, dnum, precision=HIGH)
    gkeysum = jnp.dot(dden, pos_q, precision=HIGH)
    dpos_k = (jnp.dot(v_flat, gstate.T, precision=HIGH) + gkeysum[None, :]) / TOKENS
    grad_k = jnp.where(k_flat > 0, dpos_k, 0.0)
    dv_attn = jnp.dot(pos_k, gstate, precision=HIGH) / TOKENS
    v_pad = jnp.pad(v_head.astype(jnp.float32), ((0, 0), (1, 1), (1, 1), (0, 0)))
    g_pad = jnp.pad(g_head.astype(jnp.float32), ((0, 0), (1, 1), (1, 1), (0, 0)))
    g_full = g_head.astype(jnp.float32)
    dv_conv = jnp.zeros(shape, jnp.float32)
    kernel_rows = []
    for a in (-1, 0, 1):
        kernel_cols = []
        for b in (-1, 0, 1):
            shifted = g_pad[:, 1 - a:1 - a + ROWS, 1 - b:1 - b + COLS, :]
            dv_conv = dv_conv + ker[a + 1, b + 1] * shifted
            moved = v_pad[:, 1 + a:1 + a + ROWS, 1 + b:1 + b + COLS, :]
            kernel_cols.append(jnp.sum(moved * g_full, axis=(0, 1, 2)))
        kernel_rows.append(jnp.stack(kernel_cols))
    grad_ker = jnp.stack(kernel_rows)
    grad_v = dv_attn.reshape(shape) + dv_conv
    return (grad_q.reshape(shape).astype(jnp.bfloat16), grad_k.reshape(shape).astype(jnp.bfloat16),
            grad_v.astype(jnp.bfloat16), grad_ker)


def reference(queries, keys, values, cotangent, kernel):
    def one(head):
        return head_grads(queries, keys, values, cotangent, kernel, head)

    grad_q, grad_k, grad_v, grad_ker = lax.map(one, jnp.arange(HEADS, dtype=jnp.int32))
    full = (FRAMES, ROWS, COLS, HEADS * HEAD_DIM)

    def merge(x):
        return jnp.moveaxis(x, 0, 3).reshape(full)

    grad_kernel = jnp.moveaxis(grad_ker, 0, 2).reshape(3, 3, HEADS * HEAD_DIM)
    return merge(grad_q), merge(grad_k), merge(grad_v), grad_kernel
```

```python
import functools

import jax
import jax.numpy as jnp
from jax import lax
from jax.experimental import pallas as pl
from jax.experimental.pallas import tpu as pltpu
from jax.sharding import PartitionSpec as P

MESH = pl.DeviceIdType.MESH
F32 = jnp.float32
BF16 = jnp.bfloat16

HEADS = 36
HEAD_DIM = 32
DEN_EPS = 0.1

LANES = 128
CHANNELS = HEADS * HEAD_DIM
GROUPS = CHANNELS // LANES
PACK = 16
STATE_CHUNKS = GROUPS * HEAD_DIM // PACK
ALL_CHUNKS = STATE_CHUNKS + GROUPS


def lanes(group):
    return pl.ds(group * LANES, LANES)


def block_mask():
    row = lax.broadcasted_iota(jnp.int32, (LANES, LANES), 0)
    col = lax.broadcasted_iota(jnp.int32, (LANES, LANES), 1)
    return (row // HEAD_DIM) == (col // HEAD_DIM)


def pack_heads(full):
    col = lax.broadcasted_iota(jnp.int32, (HEAD_DIM, LANES), 1) // HEAD_DIM
    out = full[0:HEAD_DIM]
    for h in range(1, LANES // HEAD_DIM):
        out = jnp.where(col == h, full[h * HEAD_DIM : (h + 1) * HEAD_DIM], out)
    return out


def unpack_heads(packed, mask):
    tiled = jnp.concatenate([packed.astype(F32)] * (LANES // HEAD_DIM), axis=0)
    return jnp.where(mask, tiled, 0.0)


def split(x):
    high = x.astype(BF16)
    return jnp.concatenate([high, (x - high.astype(F32)).astype(BF16)], axis=1)


def total(slots):
    return jnp.sum(slots.astype(F32), axis=0)


def exchange_kernel(
    sizes,
    q_hbm,
    k_hbm,
    v_hbm,
    g_hbm,
    w_hbm,
    gq_hbm,
    conv_hbm,
    sums_out,
    gks_out,
    kb,
    vb,
    qb,
    gb,
    w_ref,
    halo,
    inv_den,
    conv,
    gq,
    ks_plane,
    ks_line,
    st_src,
    st_rs,
    st_line,
    st_all,
    gs_src,
    gs_rs,
    gs_line,
    gs_all,
    gk_plane,
    gk_line,
    load_sem,
    store_sem,
    halo_send,
    halo_recv,
    send_sem,
    recv_sem,
    relay_sem,
):
    tm_size, rows_size = sizes
    plane_size, line_size = tm_size * 2, rows_size // 2
    count = kb.shape[0] * tm_size * rows_size
    width = kb.shape[0] // 2
    tm = lax.axis_index("tm")
    r = lax.axis_index("rows")
    z, core = r // 2, r % 2
    me = core * tm_size + tm

    def in_plane(i):
        return (i % tm_size, z * 2 + i // tm_size)

    def in_line(i):
        return (tm, i * 2 + core)

    loads = [
        pltpu.make_async_copy(src, dst, load_sem.at[i])
        for i, (src, dst) in enumerate(
            ((k_hbm, kb), (v_hbm, vb), (q_hbm, qb), (g_hbm, gb), (w_hbm, w_ref))
        )
    ]
    for load in loads:
        load.start()

    barrier = pltpu.get_barrier_semaphore()

    def greet(device):
        pl.semaphore_signal(barrier, inc=1, device_id=device, device_id_type=MESH)

    def greet_plane(d, _):
        greet(in_plane((me + d) % plane_size))
        return 0

    def greet_line(d, _):
        greet(in_line((z + 1 + d + (d // 4) * (line_size - 9)) % line_size))
        return 0

    lax.fori_loop(1, plane_size, greet_plane, 0)
    lax.fori_loop(0, 8, greet_line, 0)
    greet((tm, (r + 2 * core + rows_size - 1) % rows_size))

    def remote(src, dst, which, device):
        return pltpu.make_async_remote_copy(
            src_ref=src,
            dst_ref=dst,
            send_sem=send_sem.at[which],
            recv_sem=recv_sem.at[which],
            device_id=device,
            device_id_type=MESH,
        )

    def to_plane(buf, slot, which):
        def send(d, _):
            remote(buf.at[slot], buf.at[slot], which, in_plane((me + d) % plane_size)).start()
            return 0

        lax.fori_loop(1, plane_size, send, 0)

    def to_line(buf, which):
        def send(d, _):
            far = (z + line_size // 2 + (1 - 2 * (d % 2)) * ((d + 1) // 2) + line_size) % line_size
            remote(buf.at[z], buf.at[z], which, in_line(far)).start()
            return 0

        lax.fori_loop(0, line_size - 1, send, 0)

    def to_owners(src, dst, chunks, which):
        def send(i, _):
            owner = (me + i) % chunks

            @pl.when(owner != me)
            def _():
                remote(src.at[owner], dst.at[me], which, in_plane(owner)).start()

            return 0

        lax.fori_loop(0, chunks, send, 0)

        @pl.when(me < chunks)
        def _():
            dst[me] = src[me]

    def arrived(buf, n, sem):
        view = buf.at[pl.ds(0, n)]
        pltpu.make_async_copy(view, view, sem).wait()

    def all_arrived(buf, chunks, which):
        @pl.when(me < chunks)
        def _():
            arrived(buf, chunks - 1, recv_sem.at[which])

        @pl.when(me >= chunks)
        def _():
            arrived(buf, chunks, recv_sem.at[which])

    KS1, KS2, ST1, ST2, ST3, GS1, GS2, GS3, GK1, GK2 = range(10)
    mask = block_mask()
    ones_block = jnp.where(mask, 1.0, 0.0).astype(BF16)
    ones_twice = jnp.concatenate([ones_block, ones_block], axis=0)
    row16 = lax.broadcasted_iota(jnp.int32, (PACK, LANES), 0)

    loads[0].wait()
    ks_rows = jnp.zeros((PACK, LANES), F32)
    for i in range(GROUPS):
        pk = jnp.maximum(kb[:, i * LANES : (i + 1) * LANES], 0)
        ones = jnp.ones((PACK, kb.shape[0]), BF16)
        ks = jnp.dot(ones, pk, preferred_element_type=F32)
        ks_rows = jnp.where(row16 == i, ks, ks_rows)
    ks_plane[me] = ks_rows.astype(BF16)
    loads[1].wait()
    for i in range(GROUPS):
        pk = jnp.maximum(kb[:, i * LANES : (i + 1) * LANES], 0)
        full = lax.dot_general(
            pk,
            vb[:, i * LANES : (i + 1) * LANES],
            (((0,), (0,)), ((), ())),
            preferred_element_type=F32,
        )
        st_src[2 * i : 2 * i + 2] = pack_heads(full).astype(BF16).reshape(2, PACK, LANES)

    pl.semaphore_wait(barrier, plane_size + 8)
    to_plane(ks_plane, me, KS1)
    to_owners(st_src, st_rs, STATE_CHUNKS, ST1)
    for d in (4, line_size - 4):
        pl.semaphore_signal(
            relay_sem, inc=1, device_id=in_line((z + d) % line_size), device_id_type=MESH
        )

    loads[3].wait()

    def to_before():
        return pltpu.make_async_remote_copy(
            src_ref=gb.at[pl.ds(0, width)],
            dst_ref=halo.at[1],
            send_sem=halo_send.at[0],
            recv_sem=halo_recv.at[1],
            device_id=(tm, r - 1),
            device_id_type=MESH,
        )

    def to_after():
        return pltpu.make_async_remote_copy(
            src_ref=gb.at[pl.ds(width, width)],
            dst_ref=halo.at[0],
            send_sem=halo_send.at[1],
            recv_sem=halo_recv.at[0],
            device_id=(tm, r + 1),
            device_id_type=MESH,
        )

    @pl.when(r > 0)
    def _():
        to_before().start()

    @pl.when(r == 0)
    def _():
        halo[0] = jnp.zeros(halo.shape[1:], BF16)

    @pl.when(r < rows_size - 1)
    def _():
        to_after().start()

    @pl.when(r == rows_size - 1)
    def _():
        halo[1] = jnp.zeros(halo.shape[1:], BF16)

    arrived(ks_plane, plane_size - 1, recv_sem.at[KS1])
    ks_line[z] = total(ks_plane[...]).astype(BF16)
    pl.semaphore_wait(relay_sem, 2)
    to_line(ks_line, KS2)

    @pl.when(me < STATE_CHUNKS)
    def _():
        arrived(st_rs, plane_size - 1, recv_sem.at[ST1])
        st_line[z] = total(st_rs[...]).astype(BF16)
        to_line(st_line, ST2)

    @pl.when(r > 0)
    def _():
        pltpu.make_async_copy(halo.at[0], halo.at[0], halo_recv.at[0]).wait()

    @pl.when(r < rows_size - 1)
    def _():
        pltpu.make_async_copy(halo.at[1], halo.at[1], halo_recv.at[1]).wait()

    loads[4].wait()

    def conv_group(i, _):
        at = pl.ds(pl.multiple_of(i * LANES, LANES), LANES)
        col = lax.broadcasted_iota(jnp.int32, (width, LANES), 0)
        grads = (halo[0, :, at], gb[0:width, at], gb[width:, at], halo[1, :, at])
        vals = [vb[0:width, at].astype(F32), vb[width:, at].astype(F32)]
        out = [jnp.zeros((width, LANES), F32) for _ in range(2)]
        taps = [jnp.zeros((8, LANES), F32) for _ in range(9)]
        for s in range(4):
            base = grads[s].astype(F32)
            for b in (-1, 0, 1):
                if b == 1:
                    moved = jnp.where(col == 0, 0.0, pltpu.roll(base, 1, 0))
                elif b == -1:
                    moved = jnp.where(col == width - 1, 0.0, pltpu.roll(base, width - 1, 0))
                else:
                    moved = base
                for j in range(2):
                    a = j + 1 - s
                    if -1 <= a <= 1:
                        tap = (a + 1) * 3 + b + 1
                        out[j] = out[j] + w_ref[a + 1, b + 1 : b + 2, at] * moved
                        product = (vals[j] * moved).reshape(width // 8, 8, LANES)
                        taps[tap] = taps[tap] + jnp.sum(product, axis=0)
        conv[0:width, at] = out[0]
        conv[width:, at] = out[1]
        rows = jnp.zeros((PACK, LANES), F32)
        for tap in range(9):
            rows = jnp.where(row16 == tap, jnp.sum(taps[tap], axis=0, keepdims=True), rows)
        gs_src[STATE_CHUNKS + i] = rows.astype(BF16)
        return 0

    lax.fori_loop(0, GROUPS, conv_group, 0)
    conv_store = pltpu.make_async_copy(conv, conv_hbm, store_sem.at[0])
    conv_store.start()

    loads[2].wait()
    arrived(ks_line, line_size - 1, recv_sem.at[KS2])
    keysum = total(ks_line[...]) * (1.0 / count)
    for i in range(GROUPS):
        at = slice(i * LANES, (i + 1) * LANES)
        pq = jnp.maximum(qb[:, at], 0)
        weighted = split(pq.astype(F32) * keysum[i : i + 1])
        den = jnp.dot(weighted, ones_twice, preferred_element_type=F32) + DEN_EPS
        inv = 1.0 / den
        inv_den[:, at] = inv
        dnum = (gb[:, at].astype(F32) * inv).astype(BF16)
        full = lax.dot_general(
            pq, dnum, (((0,), (0,)), ((), ())), preferred_element_type=F32
        )
        gs_src[2 * i : 2 * i + 2] = pack_heads(full).astype(BF16).reshape(2, PACK, LANES)
    to_owners(gs_src, gs_rs, ALL_CHUNKS, GS1)

    @pl.when(me < STATE_CHUNKS)
    def _():
        arrived(st_line, line_size - 1, recv_sem.at[ST2])
        st_all[me] = total(st_line[...]) * (1.0 / count)
        to_plane(st_all, me, ST3)

    @pl.when(me < ALL_CHUNKS)
    def _():
        arrived(gs_rs, plane_size - 1, recv_sem.at[GS1])
        gs_line[z] = total(gs_rs[...]).astype(BF16)
        to_line(gs_line, GS2)

    all_arrived(st_all, STATE_CHUNKS, ST3)
    gks_rows = jnp.zeros((PACK, LANES), F32)
    for i in range(GROUPS):
        at = slice(i * LANES, (i + 1) * LANES)
        state = split(unpack_heads(st_all[2 * i : 2 * i + 2].reshape(HEAD_DIM, LANES), mask))
        grad = gb[:, at]
        pq = jnp.maximum(qb[:, at].astype(F32), 0.0)
        inv = inv_den[:, at]
        pulled = lax.dot_general(
            jnp.concatenate([grad, grad], axis=1),
            state,
            (((1,), (1,)), ((), ())),
            preferred_element_type=F32,
        )
        inner = jnp.dot(split(pq * pulled), ones_twice, preferred_element_type=F32)
        dden = -inner * (inv * inv)
        dq = pulled * inv + dden * keysum[i : i + 1]
        gq[:, at] = jnp.where(pq > 0, dq, 0.0).astype(BF16)
        part = jnp.sum(pq * dden, axis=0, keepdims=True)
        gks_rows = jnp.where(row16 == i, part, gks_rows)
    gk_plane[me] = gks_rows.astype(BF16)
    to_plane(gk_plane, me, GK1)
    gq_store = pltpu.make_async_copy(gq, gq_hbm, store_sem.at[1])
    gq_store.start()

    @pl.when(me < ALL_CHUNKS)
    def _():
        arrived(gs_line, line_size - 1, recv_sem.at[GS2])
        gs_all[me] = total(gs_line[...]).astype(BF16)
        to_plane(gs_all, me, GS3)

    arrived(gk_plane, plane_size - 1, recv_sem.at[GK1])
    gk_line[z] = total(gk_plane[...]).astype(BF16)
    to_line(gk_line, GK2)

    all_arrived(gs_all, ALL_CHUNKS, GS3)
    sums_out[...] = gs_all[...]
    arrived(gk_line, line_size - 1, recv_sem.at[GK2])
    gks_out[...] = total(gk_line[...])

    conv_store.wait()
    gq_store.wait()

    @pl.when(r > 0)
    def _():
        to_before().wait_send()

    @pl.when(r < rows_size - 1)
    def _():
        to_after().wait_send()

    for buf, which in ((ks_plane, KS1), (gk_plane, GK1)):
        arrived(buf, plane_size - 1, send_sem.at[which])
    for buf, which in ((ks_line, KS2), (gk_line, GK2)):
        arrived(buf, line_size - 1, send_sem.at[which])
    for chunks, src, rs, line, all_, first, second, third in (
        (STATE_CHUNKS, st_src, st_rs, st_line, st_all, ST1, ST2, ST3),
        (ALL_CHUNKS, gs_src, gs_rs, gs_line, gs_all, GS1, GS2, GS3),
    ):

        @pl.when(me < chunks)
        def _(chunks=chunks, src=src, rs=rs, line=line, all_=all_, first=first, second=second, third=third):
            arrived(src, chunks - 1, send_sem.at[first])
            arrived(line, line_size - 1, send_sem.at[second])
            for _ in range(all_.dtype.itemsize // rs.dtype.itemsize):
                arrived(rs, plane_size - 1, send_sem.at[third])

        @pl.when(me >= chunks)
        def _(chunks=chunks, src=src, first=first):
            arrived(src, chunks, send_sem.at[first])


def finish_kernel(
    count,
    k_hbm,
    v_hbm,
    conv_hbm,
    gq_hbm,
    sums,
    gks,
    gq_out,
    gk_out,
    gv_out,
    gw_out,
    kb,
    vb,
    conv,
    gk,
    gv,
    load_sem,
    store_sem,
):
    parts = 3
    wide = CHANNELS // parts
    pass_on = pltpu.make_async_copy(gq_hbm, gq_out, store_sem.at[0, parts])
    loads = []
    for p in range(parts):
        at = pl.ds(p * wide, wide)
        loads.append(
            [
                pltpu.make_async_copy(src.at[:, at], dst.at[:, at], load_sem.at[i, p])
                for i, (src, dst) in enumerate(((k_hbm, kb), (v_hbm, vb), (conv_hbm, conv)))
            ]
        )
    for part in loads:
        for load in part:
            load.start()
    pass_on.start()
    mask = block_mask()
    stores = []
    for p in range(parts):
        for load in loads[p]:
            load.wait()
        for i in range(p * (GROUPS // parts), (p + 1) * (GROUPS // parts)):
            at = slice(i * LANES, (i + 1) * LANES)
            grad = unpack_heads(sums[2 * i : 2 * i + 2].reshape(HEAD_DIM, LANES), mask).astype(BF16)
            keys = kb[:, at].astype(F32)
            dk = lax.dot_general(
                vb[:, at], grad, (((1,), (1,)), ((), ())), preferred_element_type=F32
            )
            dk = (dk + gks[i : i + 1]) * (1.0 / count)
            gk[:, at] = jnp.where(keys > 0, dk, 0.0).astype(BF16)
            dv = jnp.dot(jnp.maximum(kb[:, at], 0), grad, preferred_element_type=F32)
            gv[:, at] = (dv * (1.0 / count) + conv[:, at]).astype(BF16)
        at = pl.ds(p * wide, wide)
        for i, (src, dst) in enumerate(((gk, gk_out), (gv, gv_out))):
            store = pltpu.make_async_copy(src.at[:, at], dst.at[:, at], store_sem.at[i, p])
            store.start()
            stores.append(store)
    for i in range(GROUPS):
        at = slice(i * LANES, (i + 1) * LANES)
        rows = sums[STATE_CHUNKS + i].astype(F32)
        for a in range(3):
            gw_out[a, :, at] = rows[3 * a : 3 * a + 3]
    for store in stores:
        store.wait()
    pass_on.wait()


def shards(sizes, queries, keys, values, cotangent, kernel):
    shape = queries.shape
    tokens = shape[0] * shape[1] * shape[2]
    count = tokens * sizes[0] * sizes[1]
    flat = (tokens, CHANNELS)
    plane, line = sizes[0] * 2, sizes[1] // 2
    q, k, v, g = (x.reshape(flat) for x in (queries, keys, values, cotangent))
    q, k, v, g, w = (
        pltpu.with_memory_space_constraint(x, pltpu.HBM) for x in (q, k, v, g, kernel)
    )
    hbm = pl.BlockSpec(memory_space=pltpu.HBM)
    vmem = pl.BlockSpec(memory_space=pltpu.VMEM)

    def block(n):
        return pltpu.VMEM((n, PACK, LANES), BF16)

    gq, conv, sums, gks = pl.pallas_call(
        functools.partial(exchange_kernel, sizes),
        out_shape=(
            jax.ShapeDtypeStruct(flat, BF16),
            jax.ShapeDtypeStruct(flat, F32),
            jax.ShapeDtypeStruct((ALL_CHUNKS, PACK, LANES), BF16),
            jax.ShapeDtypeStruct((PACK, LANES), F32),
        ),
        in_specs=[hbm] * 5,
        out_specs=(hbm, hbm, vmem, vmem),
        scratch_shapes=[pltpu.VMEM(flat, BF16)] * 4
        + [
            pltpu.VMEM(kernel.shape, F32),
            pltpu.VMEM((2, tokens // 2, CHANNELS), BF16),
            pltpu.VMEM(flat, F32),
            pltpu.VMEM(flat, F32),
            pltpu.VMEM(flat, BF16),
            block(plane),
            block(line),
            block(STATE_CHUNKS),
            block(plane),
            block(line),
            pltpu.VMEM((STATE_CHUNKS, PACK, LANES), F32),
            block(ALL_CHUNKS),
            block(plane),
            block(line),
            block(ALL_CHUNKS),
            block(plane),
            block(line),
            pltpu.SemaphoreType.DMA((5,)),
            pltpu.SemaphoreType.DMA((2,)),
            pltpu.SemaphoreType.DMA((2,)),
            pltpu.SemaphoreType.DMA((2,)),
            pltpu.SemaphoreType.DMA((10,)),
            pltpu.SemaphoreType.DMA((10,)),
            pltpu.SemaphoreType.REGULAR,
        ],
        compiler_params=pltpu.CompilerParams(
            collective_id=0, has_side_effects=True, vmem_limit_bytes=48 * 1024 * 1024
        ),
    )(q, k, v, g, w)

    gq, gk, gv, gw = pl.pallas_call(
        functools.partial(finish_kernel, count),
        out_shape=(
            jax.ShapeDtypeStruct(flat, BF16),
            jax.ShapeDtypeStruct(flat, BF16),
            jax.ShapeDtypeStruct(flat, BF16),
            jax.ShapeDtypeStruct((3, 3, CHANNELS), F32),
        ),
        in_specs=[hbm] * 4 + [vmem] * 2,
        out_specs=(hbm, hbm, hbm, vmem),
        scratch_shapes=[pltpu.VMEM(flat, BF16)] * 2
        + [pltpu.VMEM(flat, F32)]
        + [pltpu.VMEM(flat, BF16)] * 2
        + [pltpu.SemaphoreType.DMA((3, 3)), pltpu.SemaphoreType.DMA((2, 4))],
        compiler_params=pltpu.CompilerParams(vmem_limit_bytes=48 * 1024 * 1024),
    )(k, v, conv, gq, sums, gks)
    return gq.reshape(shape), gk.reshape(shape), gv.reshape(shape), gw


def solution(mesh):
    sizes = (mesh.shape["tm"], mesh.shape["rows"])
    placed = P("tm", "rows", None, None)
    return jax.shard_map(
        functools.partial(shards, sizes),
        mesh=mesh,
        in_specs=(placed, placed, placed, placed, P()),
        out_specs=(placed, placed, placed, P()),
        check_vma=False,
    )
```

```python
import functools

import jax
import jax.numpy as jnp
from jax import lax
from jax.experimental import pallas as pl
from jax.experimental.pallas import tpu as pltpu
from jax.sharding import PartitionSpec as P

MESH = pl.DeviceIdType.MESH
F32 = jnp.float32
BF16 = jnp.bfloat16

HEADS = 36
HEAD_DIM = 32
DEN_EPS = 0.1

LANES = 128
CHANNELS = HEADS * HEAD_DIM
GROUPS = CHANNELS // LANES
PACK = 16
STATE_CHUNKS = GROUPS * HEAD_DIM // PACK


def lanes(group):
    return pl.ds(group * LANES, LANES)


def block_mask():
    row = lax.broadcasted_iota(jnp.int32, (LANES, LANES), 0)
    col = lax.broadcasted_iota(jnp.int32, (LANES, LANES), 1)
    return (row // HEAD_DIM) == (col // HEAD_DIM)


def pack_heads(full):
    col = lax.broadcasted_iota(jnp.int32, (HEAD_DIM, LANES), 1) // HEAD_DIM
    out = full[0:HEAD_DIM]
    for h in range(1, LANES // HEAD_DIM):
        out = jnp.where(col == h, full[h * HEAD_DIM : (h + 1) * HEAD_DIM], out)
    return out


def unpack_heads(packed, mask):
    tiled = jnp.concatenate([packed.astype(F32)] * (LANES // HEAD_DIM), axis=0)
    return jnp.where(mask, tiled, 0.0)


def split(x):
    high = x.astype(BF16)
    return jnp.concatenate([high, (x - high.astype(F32)).astype(BF16)], axis=1)


def total(slots):
    return jnp.sum(slots.astype(F32), axis=0)


def farthest_first(sizes):
    offsets = [()]
    for size in sizes:
        offsets = [o + (d,) for o in offsets for d in range(size)]
    hops = lambda o: sum(min(d, n - d) for d, n in zip(o, sizes))
    return sorted((o for o in offsets if any(o)), key=hops, reverse=True)


SIDE = 4
PLANE = 2 * SIDE * SIDE
STATE_OWNERS = 0
GRAD_OWNERS = PLANE - STATE_CHUNKS
TAP_OWNERS = 0


def exchange_kernel(
    sizes,
    q_hbm,
    k_hbm,
    v_hbm,
    g_hbm,
    w_hbm,
    gq,
    gv,
    dk,
    gw,
    kb,
    gks_out,
    conv,
    vb,
    qb,
    gb,
    w_ref,
    pq_turned,
    halo,
    inv_den,
    weight,
    ks_plane,
    ks_line,
    st_src,
    st_rs,
    st_line,
    st_all,
    st_low,
    gs_src,
    gs_rs,
    gs_line,
    gs_all,
    wk_src,
    wk_rs,
    wk_line,
    wk_all,
    gk_plane,
    gk_line,
    load_sem,
    halo_send,
    halo_recv,
    send_sem,
    recv_sem,
    relay_sem,
):
    tm_size, rows_size = sizes
    line_size = rows_size // 2
    tokens = kb.shape[0]
    count = tokens * tm_size * rows_size
    width = tokens // 2
    tm = lax.axis_index("tm")
    r = lax.axis_index("rows")
    z, core = lax.div(r, 2), lax.rem(r, 2)
    x, y = lax.div(tm, SIDE), lax.rem(tm, SIDE)
    me = core * tm_size + tm

    loads = [
        pltpu.make_async_copy(src, dst, load_sem.at[i])
        for i, (src, dst) in enumerate(
            ((k_hbm, kb), (v_hbm, vb), (q_hbm, qb), (g_hbm, gb), (w_hbm, w_ref))
        )
    ]
    loads[0].start()

    xs = [lax.rem(x + d, SIDE) * SIDE for d in range(SIDE)]
    ys = [lax.rem(y + d, SIDE) for d in range(SIDE)]
    cs = [core, 1 - core]
    plane = []
    for dx, dy, dc in farthest_first((SIDE, SIDE, 2)):
        chip = xs[dx] + ys[dy]
        plane.append((cs[dc] * tm_size + chip, (chip, 2 * z + cs[dc])))
    line = []
    for (d,) in farthest_first((line_size,)):
        line.append((tm, 2 * lax.rem(z + d, line_size) + core))
    near = line_size // 4
    barrier = pltpu.get_barrier_semaphore()

    def greet(device):
        pl.semaphore_signal(barrier, inc=1, device_id=device, device_id_type=MESH)

    def line_at(d):
        return (tm, 2 * lax.rem(z + d + line_size, line_size) + core)

    for _, device in plane:
        greet(device)
    for d in range(near, 0, -1):
        greet(line_at(d))
        greet(line_at(-d))
    greet((tm, lax.rem(r + 2 * core + rows_size - 1, rows_size)))
    for load in loads[1:]:
        load.start()

    def remote(src, dst, which, device):
        return pltpu.make_async_remote_copy(
            src_ref=src,
            dst_ref=dst,
            send_sem=send_sem.at[which],
            recv_sem=recv_sem.at[which],
            device_id=device,
            device_id_type=MESH,
        )

    def to_plane(buf, slot, which):
        for _, device in plane:
            remote(buf.at[slot], buf.at[slot], which, device).start()

    def to_line(buf, which):
        for device in line:
            remote(buf.at[z], buf.at[z], which, device).start()

    def owned(first, chunks):
        return jnp.logical_and(me >= first, me < first + chunks)

    def to_owners(src, dst, first, chunks, which):
        for index, device in plane:

            @pl.when(jnp.logical_and(index >= first, index < first + chunks))
            def _(index=index, device=device):
                remote(src.at[index - first], dst.at[me], which, device).start()

        @pl.when(owned(first, chunks))
        def _():
            dst[me] = src[me - first]

    def to_owner(src, dst, first, chunk, which):
        index = first + chunk

        @pl.when(me != index)
        def _():
            device = (index % tm_size, 2 * z + index // tm_size)
            remote(src.at[chunk], dst.at[me], which, device).start()

        @pl.when(me == index)
        def _():
            dst[me] = src[chunk]

    def arrived(buf, n, sem):
        view = buf.at[pl.ds(0, n)]
        pltpu.make_async_copy(view, view, sem).wait()

    def all_arrived(buf, first, chunks, sem):
        @pl.when(owned(first, chunks))
        def _():
            arrived(buf, chunks - 1, sem)

        @pl.when(jnp.logical_not(owned(first, chunks)))
        def _():
            arrived(buf, chunks, sem)

    KS1, KS2, ST1, ST2, ST3, ST4, GS1, GS2, GS3, WK1, WK2, WK3, GK1, GK2 = range(14)
    mask = block_mask()
    ones_block = jnp.where(mask, 1.0, 0.0).astype(BF16)
    ones_twice = jnp.concatenate([ones_block, ones_block], axis=0)
    row16 = lax.broadcasted_iota(jnp.int32, (PACK, LANES), 0)
    groups = [slice(i * LANES, (i + 1) * LANES) for i in range(GROUPS)]

    loads[0].wait()
    ks_rows = jnp.zeros((PACK, LANES), F32)
    ones = jnp.ones((PACK, tokens), BF16)
    for i, at in enumerate(groups):
        ks = jnp.dot(ones, jnp.maximum(kb[:, at], 0), preferred_element_type=F32)
        ks_rows = jnp.where(row16 == i, ks, ks_rows)
    ks_plane[me] = ks_rows.astype(BF16)
    loads[1].wait()
    for i, at in enumerate(groups):
        full = lax.dot_general(
            jnp.maximum(kb[:, at], 0),
            vb[:, at],
            (((0,), (0,)), ((), ())),
            preferred_element_type=F32,
        )
        st_src[2 * i : 2 * i + 2] = pack_heads(full).astype(BF16).reshape(2, PACK, LANES)

    pl.semaphore_wait(barrier, len(plane) + 2 * near + 1)
    to_plane(ks_plane, me, KS1)
    to_owners(st_src, st_rs, STATE_OWNERS, STATE_CHUNKS, ST1)
    for d in (near, -near):
        pl.semaphore_signal(relay_sem, inc=1, device_id=line_at(d), device_id_type=MESH)

    loads[3].wait()

    def to_before():
        return pltpu.make_async_remote_copy(
            src_ref=gb.at[pl.ds(0, width)],
            dst_ref=halo.at[1],
            send_sem=halo_send.at[0],
            recv_sem=halo_recv.at[1],
            device_id=(tm, r - 1),
            device_id_type=MESH,
        )

    def to_after():
        return pltpu.make_async_remote_copy(
            src_ref=gb.at[pl.ds(width, width)],
            dst_ref=halo.at[0],
            send_sem=halo_send.at[1],
            recv_sem=halo_recv.at[0],
            device_id=(tm, r + 1),
            device_id_type=MESH,
        )

    @pl.when(r > 0)
    def _():
        to_before().start()

    @pl.when(r == 0)
    def _():
        halo[0] = jnp.zeros(halo.shape[1:], BF16)

    @pl.when(r < rows_size - 1)
    def _():
        to_after().start()

    @pl.when(r == rows_size - 1)
    def _():
        halo[1] = jnp.zeros(halo.shape[1:], BF16)

    loads[2].wait()
    for at in groups:
        pq_turned[at, :] = jnp.maximum(qb[:, at], 0).T

    arrived(ks_plane, PLANE - 1, recv_sem.at[KS1])
    ks_line[z] = total(ks_plane[...]).astype(BF16)
    pl.semaphore_wait(relay_sem, 2)
    to_line(ks_line, KS2)

    @pl.when(owned(STATE_OWNERS, STATE_CHUNKS))
    def _():
        arrived(st_rs, PLANE - 1, recv_sem.at[ST1])
        st_line[z] = total(st_rs[...]).astype(BF16)
        to_line(st_line, ST2)

    @pl.when(r > 0)
    def _():
        pltpu.make_async_copy(halo.at[0], halo.at[0], halo_recv.at[0]).wait()

    @pl.when(r < rows_size - 1)
    def _():
        pltpu.make_async_copy(halo.at[1], halo.at[1], halo_recv.at[1]).wait()

    loads[4].wait()

    def conv_group(i, _):
        at = pl.ds(pl.multiple_of(i * LANES, LANES), LANES)
        col = lax.broadcasted_iota(jnp.int32, (width, LANES), 0)
        grads = (halo[0, :, at], gb[0:width, at], gb[width:, at], halo[1, :, at])
        vals = [vb[0:width, at].astype(F32), vb[width:, at].astype(F32)]
        out = [jnp.zeros((width, LANES), F32) for _ in range(2)]
        taps = [jnp.zeros((8, LANES), F32) for _ in range(9)]
        for s in range(4):
            base = grads[s].astype(F32)
            for b in (-1, 0, 1):
                if b == 1:
                    moved = jnp.where(col == 0, 0.0, pltpu.roll(base, 1, 0))
                elif b == -1:
                    moved = jnp.where(col == width - 1, 0.0, pltpu.roll(base, width - 1, 0))
                else:
                    moved = base
                for j in range(2):
                    a = j + 1 - s
                    if -1 <= a <= 1:
                        tap = (a + 1) * 3 + b + 1
                        out[j] = out[j] + w_ref[a + 1, b + 1 : b + 2, at] * moved
                        product = (vals[j] * moved).reshape(width // 8, 8, LANES)
                        taps[tap] = taps[tap] + jnp.sum(product, axis=0)
        conv[0:width, at] = out[0]
        conv[width:, at] = out[1]
        rows = jnp.zeros((PACK, LANES), F32)
        for tap in range(9):
            rows = jnp.where(row16 == tap, jnp.sum(taps[tap], axis=0, keepdims=True), rows)
        wk_src[i] = rows.astype(BF16)
        return 0

    lax.fori_loop(0, GROUPS, conv_group, 0)
    to_owners(wk_src, wk_rs, TAP_OWNERS, GROUPS, WK1)

    arrived(ks_line, line_size - 1, recv_sem.at[KS2])
    keysum = total(ks_line[...]) * (1.0 / count)
    for i, at in enumerate(groups):
        pq = jnp.maximum(qb[:, at], 0).astype(F32)
        weighted = split(pq * keysum[i : i + 1])
        den = jnp.dot(weighted, ones_twice, preferred_element_type=F32) + DEN_EPS
        inv = pl.reciprocal(den, approx=True)
        inv = inv * (2.0 - den * inv)
        inv_den[:, at] = inv
        dnum = (gb[:, at].astype(F32) * inv).astype(BF16)
        full = jnp.dot(pq_turned[at, :], dnum, preferred_element_type=F32)
        gs_src[2 * i : 2 * i + 2] = pack_heads(full).astype(BF16).reshape(2, PACK, LANES)
        for chunk in (2 * i, 2 * i + 1):
            to_owner(gs_src, gs_rs, GRAD_OWNERS, chunk, GS1)

    @pl.when(owned(STATE_OWNERS, STATE_CHUNKS))
    def _():
        arrived(st_line, line_size - 1, recv_sem.at[ST2])
        chunk = me - STATE_OWNERS
        state = total(st_line[...]) * (1.0 / count)
        high = state.astype(BF16)
        st_all[chunk] = high
        to_plane(st_all, chunk, ST3)
        st_low[chunk] = (state - high.astype(F32)).astype(BF16)

    for at in groups:
        inv = inv_den[:, at]
        weight[:, at] = jnp.maximum(qb[:, at].astype(F32), 0.0) * (inv * inv)

    @pl.when(owned(TAP_OWNERS, GROUPS))
    def _():
        arrived(wk_rs, PLANE - 1, recv_sem.at[WK1])
        wk_line[z] = total(wk_rs[...]).astype(BF16)
        to_line(wk_line, WK2)

    @pl.when(owned(GRAD_OWNERS, STATE_CHUNKS))
    def _():
        arrived(gs_rs, PLANE - 1, recv_sem.at[GS1])
        gs_line[z] = total(gs_rs[...]).astype(BF16)
        to_line(gs_line, GS2)

    all_arrived(st_all, STATE_OWNERS, STATE_CHUNKS, recv_sem.at[ST3])
    gk_rows = jnp.zeros((PACK, LANES), F32)
    for i, at in enumerate(groups):
        state = unpack_heads(st_all[2 * i : 2 * i + 2].reshape(HEAD_DIM, LANES), mask)
        pulled = lax.dot_general(
            gb[:, at], state.astype(BF16), (((1,), (1,)), ((), ())), preferred_element_type=F32
        )
        pq = jnp.maximum(qb[:, at].astype(F32), 0.0)
        inner = jnp.dot((pq * pulled).astype(BF16), ones_block, preferred_element_type=F32)
        part = jnp.sum(weight[:, at] * inner, axis=0, keepdims=True)
        gk_rows = jnp.where(row16 == i, -part, gk_rows)
    gk_plane[me] = gk_rows.astype(BF16)
    to_plane(gk_plane, me, GK1)

    @pl.when(owned(STATE_OWNERS, STATE_CHUNKS))
    def _():
        to_plane(st_low, me - STATE_OWNERS, ST4)

    @pl.when(owned(TAP_OWNERS, GROUPS))
    def _():
        arrived(wk_line, line_size - 1, recv_sem.at[WK2])
        chunk = me - TAP_OWNERS
        wk_all[chunk] = total(wk_line[...]).astype(BF16)
        to_plane(wk_all, chunk, WK3)

    arrived(gk_plane, PLANE - 1, recv_sem.at[GK1])
    gk_line[z] = total(gk_plane[...]).astype(BF16)
    to_line(gk_line, GK2)

    @pl.when(owned(GRAD_OWNERS, STATE_CHUNKS))
    def _():
        arrived(gs_line, line_size - 1, recv_sem.at[GS2])
        chunk = me - GRAD_OWNERS
        gs_all[chunk] = (total(gs_line[...]) * (1.0 / count)).astype(BF16)
        to_plane(gs_all, chunk, GS3)

    all_arrived(st_low, STATE_OWNERS, STATE_CHUNKS, recv_sem.at[ST4])
    for i, at in enumerate(groups):
        state = jnp.concatenate(
            [
                unpack_heads(half[2 * i : 2 * i + 2].reshape(HEAD_DIM, LANES), mask).astype(BF16)
                for half in (st_all, st_low)
            ],
            axis=1,
        )
        grad = gb[:, at]
        pulled = lax.dot_general(
            jnp.concatenate([grad, grad], axis=1),
            state,
            (((1,), (1,)), ((), ())),
            preferred_element_type=F32,
        )
        pq = jnp.maximum(qb[:, at].astype(F32), 0.0)
        inner = jnp.dot(split(pq * pulled), ones_twice, preferred_element_type=F32)
        inv = inv_den[:, at]
        dq = (pulled - inner * (inv * keysum[i : i + 1])) * inv
        gq[:, at] = jnp.where(pq > 0, dq, 0.0).astype(BF16)

    @pl.when(r > 0)
    def _():
        to_before().wait_send()

    @pl.when(r < rows_size - 1)
    def _():
        to_after().wait_send()

    for buf, which in ((ks_plane, KS1), (gk_plane, GK1)):
        arrived(buf, PLANE - 1, send_sem.at[which])
    for buf, which in ((ks_line, KS2), (gk_line, GK2)):
        arrived(buf, line_size - 1, send_sem.at[which])
    for first, chunks, src, rs, lined, steps in (
        (STATE_OWNERS, STATE_CHUNKS, st_src, st_rs, st_line, (ST1, ST2, ST3, ST4)),
        (GRAD_OWNERS, STATE_CHUNKS, gs_src, gs_rs, gs_line, (GS1, GS2, GS3)),
        (TAP_OWNERS, GROUPS, wk_src, wk_rs, wk_line, (WK1, WK2, WK3)),
    ):
        all_arrived(src, first, chunks, send_sem.at[steps[0]])

        @pl.when(owned(first, chunks))
        def _(rs=rs, lined=lined, steps=steps):
            arrived(lined, line_size - 1, send_sem.at[steps[1]])
            for step in steps[2:]:
                arrived(rs, PLANE - 1, send_sem.at[step])

    all_arrived(wk_all, TAP_OWNERS, GROUPS, recv_sem.at[WK3])
    for i, at in enumerate(groups):
        rows = wk_all[i].astype(F32)
        for a in range(3):
            gw[a, :, at] = rows[3 * a : 3 * a + 3]

    all_arrived(gs_all, GRAD_OWNERS, STATE_CHUNKS, recv_sem.at[GS3])
    for i, at in enumerate(groups):
        grad = unpack_heads(gs_all[2 * i : 2 * i + 2].reshape(HEAD_DIM, LANES), mask)
        grad = grad.astype(BF16)
        dk[:, at] = lax.dot_general(
            vb[:, at], grad, (((1,), (1,)), ((), ())), preferred_element_type=F32
        )
        dv = jnp.dot(jnp.maximum(kb[:, at], 0), grad, preferred_element_type=F32)
        gv[:, at] = (dv + conv[:, at]).astype(BF16)
    arrived(gk_line, line_size - 1, recv_sem.at[GK2])
    gks_out[...] = total(gk_line[...]) * (1.0 / count)


def finish_kernel(
    gq, gv, dk, gw, kb, gks, gq_out, gk_out, gv_out, gw_out, gk, pass_sem, store_sem
):
    stores = [
        pltpu.make_async_copy(src, dst, pass_sem.at[i])
        for i, (src, dst) in enumerate(((gq, gq_out), (gv, gv_out), (gw, gw_out)))
    ]
    for store in stores:
        store.start()
    parts = 3
    wide = CHANNELS // parts
    for p in range(parts):
        for i in range(p * (GROUPS // parts), (p + 1) * (GROUPS // parts)):
            at = slice(i * LANES, (i + 1) * LANES)
            value = dk[:, at] + gks[i : i + 1]
            gk[:, at] = jnp.where(kb[:, at].astype(F32) > 0, value, 0.0).astype(BF16)
        at = pl.ds(p * wide, wide)
        store = pltpu.make_async_copy(gk.at[:, at], gk_out.at[:, at], store_sem.at[p])
        store.start()
        stores.append(store)
    for store in stores:
        store.wait()


def shards(sizes, queries, keys, values, cotangent, kernel):
    shape = queries.shape
    tokens = shape[0] * shape[1] * shape[2]
    flat = (tokens, CHANNELS)
    line = sizes[1] // 2
    q, k, v, g = (x.reshape(flat) for x in (queries, keys, values, cotangent))
    q, k, v, g, w = (
        pltpu.with_memory_space_constraint(x, pltpu.HBM) for x in (q, k, v, g, kernel)
    )
    hbm = pl.BlockSpec(memory_space=pltpu.HBM)
    vmem = pl.BlockSpec(memory_space=pltpu.VMEM)

    def block(n):
        return pltpu.VMEM((n, PACK, LANES), BF16)

    def chain(chunks):
        return [block(chunks), block(PLANE), block(line), block(chunks)]

    gq, gv, dk, gw, kb, gks = pl.pallas_call(
        functools.partial(exchange_kernel, sizes),
        out_shape=(
            jax.ShapeDtypeStruct(flat, BF16),
            jax.ShapeDtypeStruct(flat, BF16),
            jax.ShapeDtypeStruct(flat, F32),
            jax.ShapeDtypeStruct(kernel.shape, F32),
            jax.ShapeDtypeStruct(flat, BF16),
            jax.ShapeDtypeStruct((PACK, LANES), F32),
        ),
        in_specs=[hbm] * 5,
        out_specs=(vmem,) * 6,
        scratch_shapes=[pltpu.VMEM(flat, F32)]
        + [pltpu.VMEM(flat, BF16)] * 3
        + [
            pltpu.VMEM(kernel.shape, F32),
            pltpu.VMEM((CHANNELS, tokens), BF16),
            pltpu.VMEM((2, tokens // 2, CHANNELS), BF16),
            pltpu.VMEM(flat, F32),
            pltpu.VMEM(flat, F32),
            block(PLANE),
            block(line),
        ]
        + chain(STATE_CHUNKS)
        + [block(STATE_CHUNKS)]
        + chain(STATE_CHUNKS)
        + chain(GROUPS)
        + [
            block(PLANE),
            block(line),
            pltpu.SemaphoreType.DMA((5,)),
            pltpu.SemaphoreType.DMA((2,)),
            pltpu.SemaphoreType.DMA((2,)),
            pltpu.SemaphoreType.DMA((14,)),
            pltpu.SemaphoreType.DMA((14,)),
            pltpu.SemaphoreType.REGULAR,
        ],
        compiler_params=pltpu.CompilerParams(
            collective_id=0, has_side_effects=True, vmem_limit_bytes=32 * 1024 * 1024
        ),
    )(q, k, v, g, w)

    gq, gk, gv, gw = pl.pallas_call(
        finish_kernel,
        out_shape=(
            jax.ShapeDtypeStruct(flat, BF16),
            jax.ShapeDtypeStruct(flat, BF16),
            jax.ShapeDtypeStruct(flat, BF16),
            jax.ShapeDtypeStruct((3, 3, CHANNELS), F32),
        ),
        in_specs=[vmem] * 6,
        out_specs=(hbm,) * 4,
        scratch_shapes=[
            pltpu.VMEM(flat, BF16),
            pltpu.SemaphoreType.DMA((3,)),
            pltpu.SemaphoreType.DMA((3,)),
        ],
        compiler_params=pltpu.CompilerParams(vmem_limit_bytes=32 * 1024 * 1024),
    )(gq, gv, dk, gw, kb, gks)
    return gq.reshape(shape), gk.reshape(shape), gv.reshape(shape), gw


def solution(mesh):
    sizes = (mesh.shape["tm"], mesh.shape["rows"])
    placed = P("tm", "rows", None, None)
    return jax.shard_map(
        functools.partial(shards, sizes),
        mesh=mesh,
        in_specs=(placed, placed, placed, placed, P()),
        out_specs=(placed, placed, placed, P()),
        check_vma=False,
    )
```

```python
import functools

import jax
import jax.numpy as jnp
from jax import lax
from jax.experimental import pallas as pl
from jax.experimental.pallas import tpu as pltpu
from jax.sharding import PartitionSpec as P

MESH = pl.DeviceIdType.MESH
F32 = jnp.float32
BF16 = jnp.bfloat16

HEADS = 36
HEAD_DIM = 32
DEN_EPS = 0.1

LANES = 128
CHANNELS = HEADS * HEAD_DIM
GROUPS = CHANNELS // LANES
PACK = 16
STATE_CHUNKS = GROUPS * HEAD_DIM // PACK


def lanes(group):
    return pl.ds(group * LANES, LANES)


def block_mask():
    row = lax.broadcasted_iota(jnp.int32, (LANES, LANES), 0)
    col = lax.broadcasted_iota(jnp.int32, (LANES, LANES), 1)
    return (row // HEAD_DIM) == (col // HEAD_DIM)


def pack_heads(full):
    col = lax.broadcasted_iota(jnp.int32, (HEAD_DIM, LANES), 1) // HEAD_DIM
    out = full[0:HEAD_DIM]
    for h in range(1, LANES // HEAD_DIM):
        out = jnp.where(col == h, full[h * HEAD_DIM : (h + 1) * HEAD_DIM], out)
    return out


def unpack_heads(packed, mask):
    tiled = jnp.concatenate([packed.astype(F32)] * (LANES // HEAD_DIM), axis=0)
    return jnp.where(mask, tiled, 0.0)


def split(x):
    high = x.astype(BF16)
    return jnp.concatenate([high, (x - high.astype(F32)).astype(BF16)], axis=1)


def total(slots):
    return jnp.sum(slots.astype(F32), axis=0)


def farthest_first(sizes):
    offsets = [()]
    for size in sizes:
        offsets = [o + (d,) for o in offsets for d in range(size)]
    hops = lambda o: sum(min(d, n - d) for d, n in zip(o, sizes))
    return sorted((o for o in offsets if any(o)), key=hops, reverse=True)


SIDE = 4
PLANE = 2 * SIDE * SIDE
STATE_OWNERS = 0
GRAD_OWNERS = PLANE - STATE_CHUNKS
TAP_OWNERS = 0


def exchange_kernel(
    sizes,
    q_hbm,
    k_hbm,
    v_hbm,
    g_hbm,
    w_hbm,
    gq,
    gv,
    dk,
    gw,
    kb,
    gks_out,
    conv,
    vb,
    qb,
    gb,
    w_ref,
    pq_turned,
    halo,
    inv_den,
    weight,
    ks_plane,
    ks_line,
    st_src,
    st_rs,
    st_line,
    st_all,
    st_low,
    gs_src,
    gs_rs,
    gs_line,
    gs_all,
    wk_src,
    wk_rs,
    wk_line,
    wk_all,
    gk_plane,
    gk_line,
    load_sem,
    halo_send,
    halo_recv,
    send_sem,
    recv_sem,
    relay_sem,
):
    tm_size, rows_size = sizes
    line_size = rows_size // 2
    tokens = kb.shape[0]
    count = tokens * tm_size * rows_size
    width = tokens // 2
    tm = lax.axis_index("tm")
    r = lax.axis_index("rows")
    z, core = lax.div(r, 2), lax.rem(r, 2)
    x, y = lax.div(tm, SIDE), lax.rem(tm, SIDE)
    me = core * tm_size + tm

    loads = [
        pltpu.make_async_copy(src, dst, load_sem.at[i])
        for i, (src, dst) in enumerate(
            ((k_hbm, kb), (v_hbm, vb), (q_hbm, qb), (g_hbm, gb), (w_hbm, w_ref))
        )
    ]
    loads[0].start()

    xs = [lax.rem(x + d, SIDE) * SIDE for d in range(SIDE)]
    ys = [lax.rem(y + d, SIDE) for d in range(SIDE)]
    cs = [core, 1 - core]
    plane = []
    for dx, dy, dc in farthest_first((SIDE, SIDE, 2)):
        chip = xs[dx] + ys[dy]
        plane.append((cs[dc] * tm_size + chip, (chip, 2 * z + cs[dc])))
    line = []
    for (d,) in farthest_first((line_size,)):
        line.append((tm, 2 * lax.rem(z + d, line_size) + core))
    near = line_size // 4
    barrier = pltpu.get_barrier_semaphore()

    def greet(device):
        pl.semaphore_signal(barrier, inc=1, device_id=device, device_id_type=MESH)

    def line_at(d):
        return (tm, 2 * lax.rem(z + d + line_size, line_size) + core)

    for _, device in plane:
        greet(device)
    for d in range(near, 0, -1):
        greet(line_at(d))
        greet(line_at(-d))
    greet((tm, lax.rem(r + 2 * core + rows_size - 1, rows_size)))
    for load in loads[1:]:
        load.start()

    def remote(src, dst, which, device):
        return pltpu.make_async_remote_copy(
            src_ref=src,
            dst_ref=dst,
            send_sem=send_sem.at[which],
            recv_sem=recv_sem.at[which],
            device_id=device,
            device_id_type=MESH,
        )

    def to_plane(buf, slot, which):
        for _, device in plane:
            remote(buf.at[slot], buf.at[slot], which, device).start()

    def to_line(buf, which):
        for device in line:
            remote(buf.at[z], buf.at[z], which, device).start()

    def owned(first, chunks):
        return jnp.logical_and(me >= first, me < first + chunks)

    def to_owners(src, dst, first, begin, end, which):
        n = end - begin
        mine = lax.rem(me - first - begin + PLANE, PLANE)
        start = lax.rem(mine, n)

        def send(i):
            chunk = begin + lax.rem(start + i, n)
            index = first + chunk
            device = (lax.rem(index, tm_size), 2 * z + lax.div(index, tm_size))
            remote(src.at[chunk], dst.at[me], which, device).start()

        for i in range(1, n):
            send(i)

        @pl.when(mine < n)
        def _():
            dst[me] = src[begin + start]

        @pl.when(mine >= n)
        def _():
            send(0)

    def arrived(buf, n, sem):
        view = buf.at[pl.ds(0, n)]
        pltpu.make_async_copy(view, view, sem).wait()

    def all_arrived(buf, first, chunks, sem):
        @pl.when(owned(first, chunks))
        def _():
            arrived(buf, chunks - 1, sem)

        @pl.when(jnp.logical_not(owned(first, chunks)))
        def _():
            arrived(buf, chunks, sem)

    KS1, KS2, ST1, ST2, ST3, ST4, GS1, GS2, GS3, WK1, WK2, WK3, GK1, GK2 = range(14)
    mask = block_mask()
    ones_block = jnp.where(mask, 1.0, 0.0).astype(BF16)
    ones_twice = jnp.concatenate([ones_block, ones_block], axis=0)
    row16 = lax.broadcasted_iota(jnp.int32, (PACK, LANES), 0)
    groups = [slice(i * LANES, (i + 1) * LANES) for i in range(GROUPS)]

    loads[0].wait()
    ks_rows = jnp.zeros((PACK, LANES), F32)
    ones = jnp.ones((PACK, tokens), BF16)
    for i, at in enumerate(groups):
        ks = jnp.dot(ones, jnp.maximum(kb[:, at], 0), preferred_element_type=F32)
        ks_rows = jnp.where(row16 == i, ks, ks_rows)
    ks_plane[me] = ks_rows.astype(BF16)
    loads[1].wait()
    for i, at in enumerate(groups):
        full = lax.dot_general(
            jnp.maximum(kb[:, at], 0),
            vb[:, at],
            (((0,), (0,)), ((), ())),
            preferred_element_type=F32,
        )
        st_src[2 * i : 2 * i + 2] = pack_heads(full).astype(BF16).reshape(2, PACK, LANES)

    pl.semaphore_wait(barrier, len(plane) + 2 * near + 1)
    for d in (near, -near):
        pl.semaphore_signal(relay_sem, inc=1, device_id=line_at(d), device_id_type=MESH)
    to_plane(ks_plane, me, KS1)
    to_owners(st_src, st_rs, STATE_OWNERS, 0, STATE_CHUNKS, ST1)

    loads[3].wait()

    def to_before():
        return pltpu.make_async_remote_copy(
            src_ref=gb.at[pl.ds(0, width)],
            dst_ref=halo.at[1],
            send_sem=halo_send.at[0],
            recv_sem=halo_recv.at[1],
            device_id=(tm, r - 1),
            device_id_type=MESH,
        )

    def to_after():
        return pltpu.make_async_remote_copy(
            src_ref=gb.at[pl.ds(width, width)],
            dst_ref=halo.at[0],
            send_sem=halo_send.at[1],
            recv_sem=halo_recv.at[0],
            device_id=(tm, r + 1),
            device_id_type=MESH,
        )

    @pl.when(r > 0)
    def _():
        to_before().start()

    @pl.when(r == 0)
    def _():
        halo[0] = jnp.zeros(halo.shape[1:], BF16)

    @pl.when(r < rows_size - 1)
    def _():
        to_after().start()

    @pl.when(r == rows_size - 1)
    def _():
        halo[1] = jnp.zeros(halo.shape[1:], BF16)

    loads[2].wait()
    for at in groups:
        pq_turned[at, :] = jnp.maximum(qb[:, at], 0).T

    arrived(ks_plane, PLANE - 1, recv_sem.at[KS1])
    ks_line[z] = total(ks_plane[...]).astype(BF16)
    pl.semaphore_wait(relay_sem, 2)
    to_line(ks_line, KS2)

    @pl.when(owned(STATE_OWNERS, STATE_CHUNKS))
    def _():
        arrived(st_rs, PLANE - 1, recv_sem.at[ST1])
        st_line[z] = total(st_rs[...]).astype(BF16)
        to_line(st_line, ST2)

    @pl.when(r > 0)
    def _():
        pltpu.make_async_copy(halo.at[0], halo.at[0], halo_recv.at[0]).wait()

    @pl.when(r < rows_size - 1)
    def _():
        pltpu.make_async_copy(halo.at[1], halo.at[1], halo_recv.at[1]).wait()

    loads[4].wait()

    def conv_group(i, _):
        at = pl.ds(pl.multiple_of(i * LANES, LANES), LANES)
        col = lax.broadcasted_iota(jnp.int32, (width, LANES), 0)
        grads = (halo[0, :, at], gb[0:width, at], gb[width:, at], halo[1, :, at])
        vals = [vb[0:width, at].astype(F32), vb[width:, at].astype(F32)]
        out = [jnp.zeros((width, LANES), F32) for _ in range(2)]
        taps = [jnp.zeros((8, LANES), F32) for _ in range(9)]
        for s in range(4):
            base = grads[s].astype(F32)
            for b in (-1, 0, 1):
                if b == 1:
                    moved = jnp.where(col == 0, 0.0, pltpu.roll(base, 1, 0))
                elif b == -1:
                    moved = jnp.where(col == width - 1, 0.0, pltpu.roll(base, width - 1, 0))
                else:
                    moved = base
                for j in range(2):
                    a = j + 1 - s
                    if -1 <= a <= 1:
                        tap = (a + 1) * 3 + b + 1
                        out[j] = out[j] + w_ref[a + 1, b + 1 : b + 2, at] * moved
                        product = (vals[j] * moved).reshape(width // 8, 8, LANES)
                        taps[tap] = taps[tap] + jnp.sum(product, axis=0)
        conv[0:width, at] = out[0]
        conv[width:, at] = out[1]
        rows = jnp.zeros((PACK, LANES), F32)
        for tap in range(9):
            rows = jnp.where(row16 == tap, jnp.sum(taps[tap], axis=0, keepdims=True), rows)
        wk_src[i] = rows.astype(BF16)
        return 0

    lax.fori_loop(0, GROUPS, conv_group, 0)
    to_owners(wk_src, wk_rs, TAP_OWNERS, 0, GROUPS, WK1)

    arrived(ks_line, line_size - 1, recv_sem.at[KS2])
    keysum = total(ks_line[...]) * (1.0 / count)
    for i, at in enumerate(groups):
        pq = jnp.maximum(qb[:, at], 0).astype(F32)
        weighted = split(pq * keysum[i : i + 1])
        den = jnp.dot(weighted, ones_twice, preferred_element_type=F32) + DEN_EPS
        inv = pl.reciprocal(den, approx=True)
        inv = inv * (2.0 - den * inv)
        inv_den[:, at] = inv
        dnum = (gb[:, at].astype(F32) * inv).astype(BF16)
        full = jnp.dot(pq_turned[at, :], dnum, preferred_element_type=F32)
        gs_src[2 * i : 2 * i + 2] = pack_heads(full).astype(BF16).reshape(2, PACK, LANES)
        if i % 3 == 2:
            to_owners(gs_src, gs_rs, GRAD_OWNERS, 2 * i - 4, 2 * i + 2, GS1)

    @pl.when(owned(STATE_OWNERS, STATE_CHUNKS))
    def _():
        arrived(st_line, line_size - 1, recv_sem.at[ST2])
        chunk = me - STATE_OWNERS
        state = total(st_line[...]) * (1.0 / count)
        high = state.astype(BF16)
        st_all[chunk] = high
        to_plane(st_all, chunk, ST3)
        st_low[chunk] = (state - high.astype(F32)).astype(BF16)

    for at in groups:
        inv = inv_den[:, at]
        weight[:, at] = jnp.maximum(qb[:, at].astype(F32), 0.0) * (inv * inv)

    @pl.when(owned(TAP_OWNERS, GROUPS))
    def _():
        arrived(wk_rs, PLANE - 1, recv_sem.at[WK1])
        wk_line[z] = total(wk_rs[...]).astype(BF16)
        to_line(wk_line, WK2)

    @pl.when(owned(STATE_OWNERS, STATE_CHUNKS))
    def _():
        to_plane(st_low, me - STATE_OWNERS, ST4)

    @pl.when(owned(GRAD_OWNERS, STATE_CHUNKS))
    def _():
        arrived(gs_rs, PLANE - 1, recv_sem.at[GS1])
        gs_line[z] = total(gs_rs[...]).astype(BF16)
        to_line(gs_line, GS2)

    all_arrived(st_all, STATE_OWNERS, STATE_CHUNKS, recv_sem.at[ST3])
    gk_rows = jnp.zeros((PACK, LANES), F32)
    for i, at in enumerate(groups):
        state = unpack_heads(st_all[2 * i : 2 * i + 2].reshape(HEAD_DIM, LANES), mask)
        pulled = lax.dot_general(
            gb[:, at], state.astype(BF16), (((1,), (1,)), ((), ())), preferred_element_type=F32
        )
        pq = jnp.maximum(qb[:, at].astype(F32), 0.0)
        inner = jnp.dot((pq * pulled).astype(BF16), ones_block, preferred_element_type=F32)
        part = jnp.sum(weight[:, at] * inner, axis=0, keepdims=True)
        gk_rows = jnp.where(row16 == i, -part, gk_rows)
    gk_plane[me] = gk_rows.astype(BF16)
    to_plane(gk_plane, me, GK1)

    all_arrived(st_low, STATE_OWNERS, STATE_CHUNKS, recv_sem.at[ST4])
    for i, at in enumerate(groups):
        state = jnp.concatenate(
            [
                unpack_heads(half[2 * i : 2 * i + 2].reshape(HEAD_DIM, LANES), mask).astype(BF16)
                for half in (st_all, st_low)
            ],
            axis=1,
        )
        grad = gb[:, at]
        pulled = lax.dot_general(
            jnp.concatenate([grad, grad], axis=1),
            state,
            (((1,), (1,)), ((), ())),
            preferred_element_type=F32,
        )
        pq = jnp.maximum(qb[:, at].astype(F32), 0.0)
        inner = jnp.dot(split(pq * pulled), ones_twice, preferred_element_type=F32)
        inv = inv_den[:, at]
        dq = (pulled - inner * (inv * keysum[i : i + 1])) * inv
        gq[:, at] = jnp.where(pq > 0, dq, 0.0).astype(BF16)

    @pl.when(owned(TAP_OWNERS, GROUPS))
    def _():
        arrived(wk_line, line_size - 1, recv_sem.at[WK2])
        chunk = me - TAP_OWNERS
        wk_all[chunk] = total(wk_line[...]).astype(BF16)
        to_plane(wk_all, chunk, WK3)

    arrived(gk_plane, PLANE - 1, recv_sem.at[GK1])
    gk_line[z] = total(gk_plane[...]).astype(BF16)
    to_line(gk_line, GK2)

    @pl.when(owned(GRAD_OWNERS, STATE_CHUNKS))
    def _():
        arrived(gs_line, line_size - 1, recv_sem.at[GS2])
        chunk = me - GRAD_OWNERS
        gs_all[chunk] = (total(gs_line[...]) * (1.0 / count)).astype(BF16)
        to_plane(gs_all, chunk, GS3)

    @pl.when(r > 0)
    def _():
        to_before().wait_send()

    @pl.when(r < rows_size - 1)
    def _():
        to_after().wait_send()

    for buf, which in ((ks_plane, KS1), (gk_plane, GK1)):
        arrived(buf, PLANE - 1, send_sem.at[which])
    for buf, which in ((ks_line, KS2), (gk_line, GK2)):
        arrived(buf, line_size - 1, send_sem.at[which])
    for first, chunks, src, rs, lined, steps in (
        (STATE_OWNERS, STATE_CHUNKS, st_src, st_rs, st_line, (ST1, ST2, ST3, ST4)),
        (GRAD_OWNERS, STATE_CHUNKS, gs_src, gs_rs, gs_line, (GS1, GS2, GS3)),
        (TAP_OWNERS, GROUPS, wk_src, wk_rs, wk_line, (WK1, WK2, WK3)),
    ):
        all_arrived(src, first, chunks, send_sem.at[steps[0]])

        @pl.when(owned(first, chunks))
        def _(rs=rs, lined=lined, steps=steps):
            arrived(lined, line_size - 1, send_sem.at[steps[1]])
            for step in steps[2:]:
                arrived(rs, PLANE - 1, send_sem.at[step])

    all_arrived(wk_all, TAP_OWNERS, GROUPS, recv_sem.at[WK3])
    for i, at in enumerate(groups):
        rows = wk_all[i].astype(F32)
        for a in range(3):
            gw[a, :, at] = rows[3 * a : 3 * a + 3]

    all_arrived(gs_all, GRAD_OWNERS, STATE_CHUNKS, recv_sem.at[GS3])
    for i, at in enumerate(groups):
        grad = unpack_heads(gs_all[2 * i : 2 * i + 2].reshape(HEAD_DIM, LANES), mask)
        grad = grad.astype(BF16)
        dk[:, at] = lax.dot_general(
            vb[:, at], grad, (((1,), (1,)), ((), ())), preferred_element_type=F32
        )
        dv = jnp.dot(jnp.maximum(kb[:, at], 0), grad, preferred_element_type=F32)
        gv[:, at] = (dv + conv[:, at]).astype(BF16)
    arrived(gk_line, line_size - 1, recv_sem.at[GK2])
    gks_out[...] = total(gk_line[...]) * (1.0 / count)


def finish_kernel(
    gq, gv, dk, gw, kb, gks, gq_out, gk_out, gv_out, gw_out, gk, pass_sem, store_sem
):
    stores = [
        pltpu.make_async_copy(src, dst, pass_sem.at[i])
        for i, (src, dst) in enumerate(((gq, gq_out), (gv, gv_out), (gw, gw_out)))
    ]
    for store in stores:
        store.start()
    parts = 3
    wide = CHANNELS // parts
    for p in range(parts):
        for i in range(p * (GROUPS // parts), (p + 1) * (GROUPS // parts)):
            at = slice(i * LANES, (i + 1) * LANES)
            value = dk[:, at] + gks[i : i + 1]
            gk[:, at] = jnp.where(kb[:, at].astype(F32) > 0, value, 0.0).astype(BF16)
        at = pl.ds(p * wide, wide)
        store = pltpu.make_async_copy(gk.at[:, at], gk_out.at[:, at], store_sem.at[p])
        store.start()
        stores.append(store)
    for store in stores:
        store.wait()


def shards(sizes, queries, keys, values, cotangent, kernel):
    shape = queries.shape
    tokens = shape[0] * shape[1] * shape[2]
    flat = (tokens, CHANNELS)
    line = sizes[1] // 2
    q, k, v, g = (x.reshape(flat) for x in (queries, keys, values, cotangent))
    q, k, v, g, w = (
        pltpu.with_memory_space_constraint(x, pltpu.HBM) for x in (q, k, v, g, kernel)
    )
    hbm = pl.BlockSpec(memory_space=pltpu.HBM)
    vmem = pl.BlockSpec(memory_space=pltpu.VMEM)

    def block(n):
        return pltpu.VMEM((n, PACK, LANES), BF16)

    def chain(chunks):
        return [block(chunks), block(PLANE), block(line), block(chunks)]

    gq, gv, dk, gw, kb, gks = pl.pallas_call(
        functools.partial(exchange_kernel, sizes),
        out_shape=(
            jax.ShapeDtypeStruct(flat, BF16),
            jax.ShapeDtypeStruct(flat, BF16),
            jax.ShapeDtypeStruct(flat, F32),
            jax.ShapeDtypeStruct(kernel.shape, F32),
            jax.ShapeDtypeStruct(flat, BF16),
            jax.ShapeDtypeStruct((PACK, LANES), F32),
        ),
        in_specs=[hbm] * 5,
        out_specs=(vmem,) * 6,
        scratch_shapes=[pltpu.VMEM(flat, F32)]
        + [pltpu.VMEM(flat, BF16)] * 3
        + [
            pltpu.VMEM(kernel.shape, F32),
            pltpu.VMEM((CHANNELS, tokens), BF16),
            pltpu.VMEM((2, tokens // 2, CHANNELS), BF16),
            pltpu.VMEM(flat, F32),
            pltpu.VMEM(flat, F32),
            block(PLANE),
            block(line),
        ]
        + chain(STATE_CHUNKS)
        + [block(STATE_CHUNKS)]
        + chain(STATE_CHUNKS)
        + chain(GROUPS)
        + [
            block(PLANE),
            block(line),
            pltpu.SemaphoreType.DMA((5,)),
            pltpu.SemaphoreType.DMA((2,)),
            pltpu.SemaphoreType.DMA((2,)),
            pltpu.SemaphoreType.DMA((14,)),
            pltpu.SemaphoreType.DMA((14,)),
            pltpu.SemaphoreType.REGULAR,
        ],
        compiler_params=pltpu.CompilerParams(
            collective_id=0, has_side_effects=True, vmem_limit_bytes=32 * 1024 * 1024
        ),
    )(q, k, v, g, w)

    gq, gk, gv, gw = pl.pallas_call(
        finish_kernel,
        out_shape=(
            jax.ShapeDtypeStruct(flat, BF16),
            jax.ShapeDtypeStruct(flat, BF16),
            jax.ShapeDtypeStruct(flat, BF16),
            jax.ShapeDtypeStruct((3, 3, CHANNELS), F32),
        ),
        in_specs=[vmem] * 6,
        out_specs=(hbm,) * 4,
        scratch_shapes=[
            pltpu.VMEM(flat, BF16),
            pltpu.SemaphoreType.DMA((3,)),
            pltpu.SemaphoreType.DMA((3,)),
        ],
        compiler_params=pltpu.CompilerParams(vmem_limit_bytes=32 * 1024 * 1024),
    )(gq, gv, dk, gw, kb, gks)
    return gq.reshape(shape), gk.reshape(shape), gv.reshape(shape), gw


def solution(mesh):
    sizes = (mesh.shape["tm"], mesh.shape["rows"])
    placed = P("tm", "rows", None, None)
    return jax.shard_map(
        functools.partial(shards, sizes),
        mesh=mesh,
        in_specs=(placed, placed, placed, placed, P()),
        out_specs=(placed, placed, placed, P()),
        check_vma=False,
    )
```

```python
import functools

import jax
import jax.numpy as jnp
from jax import lax
from jax.experimental import pallas as pl
from jax.experimental.pallas import tpu as pltpu
from jax.sharding import PartitionSpec as P

MESH = pl.DeviceIdType.MESH
F32 = jnp.float32
BF16 = jnp.bfloat16

HEADS = 36
HEAD_DIM = 32
DEN_EPS = 0.1

LANES = 128
CHANNELS = HEADS * HEAD_DIM
GROUPS = CHANNELS // LANES
PACK = 16
STATE_CHUNKS = GROUPS * HEAD_DIM // PACK


def lanes(group):
    return pl.ds(group * LANES, LANES)


def block_mask():
    row = lax.broadcasted_iota(jnp.int32, (LANES, LANES), 0)
    col = lax.broadcasted_iota(jnp.int32, (LANES, LANES), 1)
    return (row // HEAD_DIM) == (col // HEAD_DIM)


def pack_heads(full):
    col = lax.broadcasted_iota(jnp.int32, (HEAD_DIM, LANES), 1) // HEAD_DIM
    out = full[0:HEAD_DIM]
    for h in range(1, LANES // HEAD_DIM):
        out = jnp.where(col == h, full[h * HEAD_DIM : (h + 1) * HEAD_DIM], out)
    return out


def unpack_heads(packed, mask):
    tiled = jnp.concatenate([packed.astype(F32)] * (LANES // HEAD_DIM), axis=0)
    return jnp.where(mask, tiled, 0.0)


def split(x):
    high = x.astype(BF16)
    return jnp.concatenate([high, (x - high.astype(F32)).astype(BF16)], axis=1)


def total(slots):
    return jnp.sum(slots.astype(F32), axis=0)


def farthest_first(sizes):
    offsets = [()]
    for size in sizes:
        offsets = [o + (d,) for o in offsets for d in range(size)]
    hops = lambda o: sum(min(d, n - d) for d, n in zip(o, sizes))
    return sorted((o for o in offsets if any(o)), key=hops, reverse=True)


SIDE = 4
PLANE = 2 * SIDE * SIDE
STATE_OWNERS = 0
GRAD_OWNERS = PLANE - STATE_CHUNKS
TAP_OWNERS = 0


def exchange_kernel(
    sizes,
    q_hbm,
    k_hbm,
    v_hbm,
    g_hbm,
    w_hbm,
    gq,
    gv,
    dk,
    gw,
    kb,
    gks_out,
    conv,
    vb,
    qb,
    gb,
    w_ref,
    pq_turned,
    halo,
    inv_den,
    weight,
    ks_plane,
    ks_line,
    st_src,
    st_rs,
    st_line,
    st_all,
    st_low,
    gs_src,
    gs_rs,
    gs_line,
    gs_all,
    wk_src,
    wk_rs,
    wk_line,
    wk_all,
    gk_plane,
    gk_line,
    load_sem,
    halo_send,
    halo_recv,
    send_sem,
    recv_sem,
    relay_sem,
):
    tm_size, rows_size = sizes
    line_size = rows_size // 2
    tokens = kb.shape[0]
    count = tokens * tm_size * rows_size
    width = tokens // 2
    tm = lax.axis_index("tm")
    r = lax.axis_index("rows")
    z, core = lax.div(r, 2), lax.rem(r, 2)
    x, y = lax.div(tm, SIDE), lax.rem(tm, SIDE)
    me = core * tm_size + tm

    loads = [
        pltpu.make_async_copy(src, dst, load_sem.at[i])
        for i, (src, dst) in enumerate(
            ((k_hbm, kb), (v_hbm, vb), (q_hbm, qb), (g_hbm, gb), (w_hbm, w_ref))
        )
    ]
    loads[0].start()

    xs = [lax.rem(x + d, SIDE) * SIDE for d in range(SIDE)]
    ys = [lax.rem(y + d, SIDE) for d in range(SIDE)]
    cs = [core, 1 - core]
    plane = []
    for dx, dy, dc in farthest_first((SIDE, SIDE, 2)):
        chip = xs[dx] + ys[dy]
        plane.append((cs[dc] * tm_size + chip, (chip, 2 * z + cs[dc])))
    line = []
    for (d,) in farthest_first((line_size,)):
        line.append((tm, 2 * lax.rem(z + d, line_size) + core))
    near = line_size // 4
    barrier = pltpu.get_barrier_semaphore()

    def greet(device):
        pl.semaphore_signal(barrier, inc=1, device_id=device, device_id_type=MESH)

    def line_at(d):
        return (tm, 2 * lax.rem(z + d + line_size, line_size) + core)

    for _, device in plane:
        greet(device)
    for d in range(near, 0, -1):
        greet(line_at(d))
        greet(line_at(-d))
    greet((tm, lax.rem(r + 2 * core + rows_size - 1, rows_size)))
    for load in loads[1:]:
        load.start()

    def remote(src, dst, which, device):
        return pltpu.make_async_remote_copy(
            src_ref=src,
            dst_ref=dst,
            send_sem=send_sem.at[which],
            recv_sem=recv_sem.at[which],
            device_id=device,
            device_id_type=MESH,
        )

    def to_plane(buf, slot, which):
        for _, device in plane:
            remote(buf.at[slot], buf.at[slot], which, device).start()

    def to_line(buf, which):
        for device in line:
            remote(buf.at[z], buf.at[z], which, device).start()

    def owned(first, chunks):
        return jnp.logical_and(me >= first, me < first + chunks)

    def to_owners(src, dst, first, begin, end, which):
        n = end - begin
        mine = lax.rem(me - first - begin + PLANE, PLANE)
        start = lax.rem(mine, n)

        def send(i):
            chunk = begin + lax.rem(start + i, n)
            index = first + chunk
            device = (lax.rem(index, tm_size), 2 * z + lax.div(index, tm_size))
            remote(src.at[chunk], dst.at[me], which, device).start()

        for i in range(1, n):
            send(i)

        @pl.when(mine < n)
        def _():
            dst[me] = src[begin + start]

        @pl.when(mine >= n)
        def _():
            send(0)

    def arrived(buf, n, sem):
        view = buf.at[pl.ds(0, n)]
        pltpu.make_async_copy(view, view, sem).wait()

    def all_arrived(buf, first, chunks, sem):
        @pl.when(owned(first, chunks))
        def _():
            arrived(buf, chunks - 1, sem)

        @pl.when(jnp.logical_not(owned(first, chunks)))
        def _():
            arrived(buf, chunks, sem)

    KS1, KS2, ST1, ST2, ST3, ST4, GS1, GS2, GS3, WK1, WK2, WK3, GK1, GK2 = range(14)
    mask = block_mask()
    ones_block = jnp.where(mask, 1.0, 0.0).astype(BF16)
    ones_twice = jnp.concatenate([ones_block, ones_block], axis=0)
    row16 = lax.broadcasted_iota(jnp.int32, (PACK, LANES), 0)
    groups = [slice(i * LANES, (i + 1) * LANES) for i in range(GROUPS)]

    loads[0].wait()
    ks_rows = jnp.zeros((PACK, LANES), F32)
    ones = jnp.ones((PACK, tokens), BF16)
    for i, at in enumerate(groups):
        ks = jnp.dot(ones, jnp.maximum(kb[:, at], 0), preferred_element_type=F32)
        ks_rows = jnp.where(row16 == i, ks, ks_rows)
    ks_plane[me] = ks_rows.astype(BF16)
    loads[1].wait()
    for i, at in enumerate(groups):
        full = lax.dot_general(
            jnp.maximum(kb[:, at], 0),
            vb[:, at],
            (((0,), (0,)), ((), ())),
            preferred_element_type=F32,
        )
        st_src[2 * i : 2 * i + 2] = pack_heads(full).astype(BF16).reshape(2, PACK, LANES)

    pl.semaphore_wait(barrier, len(plane) + 2 * near + 1)
    for d in (near, -near):
        pl.semaphore_signal(relay_sem, inc=1, device_id=line_at(d), device_id_type=MESH)
    to_plane(ks_plane, me, KS1)
    to_owners(st_src, st_rs, STATE_OWNERS, 0, STATE_CHUNKS, ST1)

    loads[3].wait()

    def to_before():
        return pltpu.make_async_remote_copy(
            src_ref=gb.at[pl.ds(0, width)],
            dst_ref=halo.at[1],
            send_sem=halo_send.at[0],
            recv_sem=halo_recv.at[1],
            device_id=(tm, r - 1),
            device_id_type=MESH,
        )

    def to_after():
        return pltpu.make_async_remote_copy(
            src_ref=gb.at[pl.ds(width, width)],
            dst_ref=halo.at[0],
            send_sem=halo_send.at[1],
            recv_sem=halo_recv.at[0],
            device_id=(tm, r + 1),
            device_id_type=MESH,
        )

    @pl.when(r > 0)
    def _():
        to_before().start()

    @pl.when(r == 0)
    def _():
        halo[0] = jnp.zeros(halo.shape[1:], BF16)

    @pl.when(r < rows_size - 1)
    def _():
        to_after().start()

    @pl.when(r == rows_size - 1)
    def _():
        halo[1] = jnp.zeros(halo.shape[1:], BF16)

    loads[2].wait()
    for at in groups:
        pq = jnp.maximum(qb[:, at], 0)
        pq_turned[at, :] = pq.T
        weight[:, at] = pq.astype(F32)

    arrived(ks_plane, PLANE - 1, recv_sem.at[KS1])
    ks_line[z] = total(ks_plane[...]).astype(BF16)
    pl.semaphore_wait(relay_sem, 2)
    to_line(ks_line, KS2)

    @pl.when(owned(STATE_OWNERS, STATE_CHUNKS))
    def _():
        arrived(st_rs, PLANE - 1, recv_sem.at[ST1])
        st_line[z] = total(st_rs[...]).astype(BF16)
        to_line(st_line, ST2)

    @pl.when(r > 0)
    def _():
        pltpu.make_async_copy(halo.at[0], halo.at[0], halo_recv.at[0]).wait()

    @pl.when(r < rows_size - 1)
    def _():
        pltpu.make_async_copy(halo.at[1], halo.at[1], halo_recv.at[1]).wait()

    loads[4].wait()

    def conv_group(i, _):
        at = pl.ds(pl.multiple_of(i * LANES, LANES), LANES)
        col = lax.broadcasted_iota(jnp.int32, (width, LANES), 0)
        grads = (halo[0, :, at], gb[0:width, at], gb[width:, at], halo[1, :, at])
        vals = [vb[0:width, at].astype(F32), vb[width:, at].astype(F32)]
        out = [jnp.zeros((width, LANES), F32) for _ in range(2)]
        taps = [jnp.zeros((8, LANES), F32) for _ in range(9)]
        for s in range(4):
            base = grads[s].astype(F32)
            for b in (-1, 0, 1):
                if b == 1:
                    moved = jnp.where(col == 0, 0.0, pltpu.roll(base, 1, 0))
                elif b == -1:
                    moved = jnp.where(col == width - 1, 0.0, pltpu.roll(base, width - 1, 0))
                else:
                    moved = base
                for j in range(2):
                    a = j + 1 - s
                    if -1 <= a <= 1:
                        tap = (a + 1) * 3 + b + 1
                        out[j] = out[j] + w_ref[a + 1, b + 1 : b + 2, at] * moved
                        product = (vals[j] * moved).reshape(width // 8, 8, LANES)
                        taps[tap] = taps[tap] + jnp.sum(product, axis=0)
        conv[0:width, at] = out[0]
        conv[width:, at] = out[1]
        rows = jnp.zeros((PACK, LANES), F32)
        for tap in range(9):
            rows = jnp.where(row16 == tap, jnp.sum(taps[tap], axis=0, keepdims=True), rows)
        wk_src[i] = rows.astype(BF16)
        return 0

    lax.fori_loop(0, GROUPS, conv_group, 0)
    to_owners(wk_src, wk_rs, TAP_OWNERS, 0, GROUPS, WK1)

    arrived(ks_line, line_size - 1, recv_sem.at[KS2])
    keysum = total(ks_line[...]) * (1.0 / count)
    for i, at in enumerate(groups):
        weighted = split(weight[:, at] * keysum[i : i + 1])
        den = jnp.dot(weighted, ones_twice, preferred_element_type=F32) + DEN_EPS
        inv = pl.reciprocal(den, approx=True)
        inv = inv * (2.0 - den * inv)
        inv_den[:, at] = inv
        dnum = (gb[:, at].astype(F32) * inv).astype(BF16)
        full = jnp.dot(pq_turned[at, :], dnum, preferred_element_type=F32)
        gs_src[2 * i : 2 * i + 2] = pack_heads(full).astype(BF16).reshape(2, PACK, LANES)
        if i % 3 == 2:
            to_owners(gs_src, gs_rs, GRAD_OWNERS, 2 * i - 4, 2 * i + 2, GS1)

    @pl.when(owned(STATE_OWNERS, STATE_CHUNKS))
    def _():
        arrived(st_line, line_size - 1, recv_sem.at[ST2])
        chunk = me - STATE_OWNERS
        state = total(st_line[...]) * (1.0 / count)
        high = state.astype(BF16)
        st_all[chunk] = high
        to_plane(st_all, chunk, ST3)
        st_low[chunk] = (state - high.astype(F32)).astype(BF16)

    for at in groups:
        inv = inv_den[:, at]
        weight[:, at] = weight[:, at] * (inv * inv)

    @pl.when(owned(TAP_OWNERS, GROUPS))
    def _():
        arrived(wk_rs, PLANE - 1, recv_sem.at[WK1])
        wk_line[z] = total(wk_rs[...]).astype(BF16)
        to_line(wk_line, WK2)

    @pl.when(owned(STATE_OWNERS, STATE_CHUNKS))
    def _():
        to_plane(st_low, me - STATE_OWNERS, ST4)

    @pl.when(owned(GRAD_OWNERS, STATE_CHUNKS))
    def _():
        arrived(gs_rs, PLANE - 1, recv_sem.at[GS1])
        gs_line[z] = total(gs_rs[...]).astype(BF16)
        to_line(gs_line, GS2)

    all_arrived(st_all, STATE_OWNERS, STATE_CHUNKS, recv_sem.at[ST3])
    gk_rows = jnp.zeros((PACK, LANES), F32)
    for i, at in enumerate(groups):
        state = unpack_heads(st_all[2 * i : 2 * i + 2].reshape(HEAD_DIM, LANES), mask)
        pulled = lax.dot_general(
            gb[:, at], state.astype(BF16), (((1,), (1,)), ((), ())), preferred_element_type=F32
        )
        pq = jnp.maximum(qb[:, at].astype(F32), 0.0)
        inner = jnp.dot((pq * pulled).astype(BF16), ones_block, preferred_element_type=F32)
        part = jnp.sum(weight[:, at] * inner, axis=0, keepdims=True)
        gk_rows = jnp.where(row16 == i, -part, gk_rows)
    gk_plane[me] = gk_rows.astype(BF16)
    to_plane(gk_plane, me, GK1)

    all_arrived(st_low, STATE_OWNERS, STATE_CHUNKS, recv_sem.at[ST4])
    for i, at in enumerate(groups):
        state = jnp.concatenate(
            [
                unpack_heads(half[2 * i : 2 * i + 2].reshape(HEAD_DIM, LANES), mask).astype(BF16)
                for half in (st_all, st_low)
            ],
            axis=1,
        )
        grad = gb[:, at]
        pulled = lax.dot_general(
            jnp.concatenate([grad, grad], axis=1),
            state,
            (((1,), (1,)), ((), ())),
            preferred_element_type=F32,
        )
        pq = jnp.maximum(qb[:, at].astype(F32), 0.0)
        inner = jnp.dot(split(pq * pulled), ones_twice, preferred_element_type=F32)
        inv = inv_den[:, at]
        dq = (pulled - inner * (inv * keysum[i : i + 1])) * inv
        gq[:, at] = jnp.where(pq > 0, dq, 0.0).astype(BF16)

    @pl.when(owned(TAP_OWNERS, GROUPS))
    def _():
        arrived(wk_line, line_size - 1, recv_sem.at[WK2])
        chunk = me - TAP_OWNERS
        wk_all[chunk] = total(wk_line[...]).astype(BF16)
        to_plane(wk_all, chunk, WK3)

    arrived(gk_plane, PLANE - 1, recv_sem.at[GK1])
    gk_line[z] = total(gk_plane[...]).astype(BF16)
    to_line(gk_line, GK2)

    @pl.when(owned(GRAD_OWNERS, STATE_CHUNKS))
    def _():
        arrived(gs_line, line_size - 1, recv_sem.at[GS2])
        chunk = me - GRAD_OWNERS
        gs_all[chunk] = (total(gs_line[...]) * (1.0 / count)).astype(BF16)
        to_plane(gs_all, chunk, GS3)

    @pl.when(r > 0)
    def _():
        to_before().wait_send()

    @pl.when(r < rows_size - 1)
    def _():
        to_after().wait_send()

    for buf, which in ((ks_plane, KS1), (gk_plane, GK1)):
        arrived(buf, PLANE - 1, send_sem.at[which])
    for buf, which in ((ks_line, KS2), (gk_line, GK2)):
        arrived(buf, line_size - 1, send_sem.at[which])
    for first, chunks, src, rs, lined, steps in (
        (STATE_OWNERS, STATE_CHUNKS, st_src, st_rs, st_line, (ST1, ST2, ST3, ST4)),
        (GRAD_OWNERS, STATE_CHUNKS, gs_src, gs_rs, gs_line, (GS1, GS2, GS3)),
        (TAP_OWNERS, GROUPS, wk_src, wk_rs, wk_line, (WK1, WK2, WK3)),
    ):
        all_arrived(src, first, chunks, send_sem.at[steps[0]])

        @pl.when(owned(first, chunks))
        def _(rs=rs, lined=lined, steps=steps):
            arrived(lined, line_size - 1, send_sem.at[steps[1]])
            for step in steps[2:]:
                arrived(rs, PLANE - 1, send_sem.at[step])

    all_arrived(wk_all, TAP_OWNERS, GROUPS, recv_sem.at[WK3])
    for i, at in enumerate(groups):
        rows = wk_all[i].astype(F32)
        for a in range(3):
            gw[a, :, at] = rows[3 * a : 3 * a + 3]

    all_arrived(gs_all, GRAD_OWNERS, STATE_CHUNKS, recv_sem.at[GS3])
    for i, at in enumerate(groups):
        grad = unpack_heads(gs_all[2 * i : 2 * i + 2].reshape(HEAD_DIM, LANES), mask)
        grad = grad.astype(BF16)
        dk[:, at] = lax.dot_general(
            vb[:, at], grad, (((1,), (1,)), ((), ())), preferred_element_type=F32
        )
        dv = jnp.dot(jnp.maximum(kb[:, at], 0), grad, preferred_element_type=F32)
        gv[:, at] = (dv + conv[:, at]).astype(BF16)
    arrived(gk_line, line_size - 1, recv_sem.at[GK2])
    gks_out[...] = total(gk_line[...]) * (1.0 / count)


def finish_kernel(
    gq, gv, dk, gw, kb, gks, gq_out, gk_out, gv_out, gw_out, gk, pass_sem, store_sem
):
    stores = [
        pltpu.make_async_copy(src, dst, pass_sem.at[i])
        for i, (src, dst) in enumerate(((gq, gq_out), (gv, gv_out), (gw, gw_out)))
    ]
    for store in stores:
        store.start()
    parts = 1
    wide = CHANNELS // parts
    for p in range(parts):
        for i in range(p * (GROUPS // parts), (p + 1) * (GROUPS // parts)):
            at = slice(i * LANES, (i + 1) * LANES)
            value = dk[:, at] + gks[i : i + 1]
            gk[:, at] = jnp.where(kb[:, at].astype(F32) > 0, value, 0.0).astype(BF16)
        at = pl.ds(p * wide, wide)
        store = pltpu.make_async_copy(gk.at[:, at], gk_out.at[:, at], store_sem.at[p])
        store.start()
        stores.append(store)
    for store in stores:
        store.wait()


def shards(sizes, queries, keys, values, cotangent, kernel):
    shape = queries.shape
    tokens = shape[0] * shape[1] * shape[2]
    flat = (tokens, CHANNELS)
    line = sizes[1] // 2
    q, k, v, g = (x.reshape(flat) for x in (queries, keys, values, cotangent))
    q, k, v, g, w = (
        pltpu.with_memory_space_constraint(x, pltpu.HBM) for x in (q, k, v, g, kernel)
    )
    hbm = pl.BlockSpec(memory_space=pltpu.HBM)
    vmem = pl.BlockSpec(memory_space=pltpu.VMEM)

    def block(n):
        return pltpu.VMEM((n, PACK, LANES), BF16)

    def chain(chunks):
        return [block(chunks), block(PLANE), block(line), block(chunks)]

    gq, gv, dk, gw, kb, gks = pl.pallas_call(
        functools.partial(exchange_kernel, sizes),
        out_shape=(
            jax.ShapeDtypeStruct(flat, BF16),
            jax.ShapeDtypeStruct(flat, BF16),
            jax.ShapeDtypeStruct(flat, F32),
            jax.ShapeDtypeStruct(kernel.shape, F32),
            jax.ShapeDtypeStruct(flat, BF16),
            jax.ShapeDtypeStruct((PACK, LANES), F32),
        ),
        in_specs=[hbm] * 5,
        out_specs=(vmem,) * 6,
        scratch_shapes=[pltpu.VMEM(flat, F32)]
        + [pltpu.VMEM(flat, BF16)] * 3
        + [
            pltpu.VMEM(kernel.shape, F32),
            pltpu.VMEM((CHANNELS, tokens), BF16),
            pltpu.VMEM((2, tokens // 2, CHANNELS), BF16),
            pltpu.VMEM(flat, F32),
            pltpu.VMEM(flat, F32),
            block(PLANE),
            block(line),
        ]
        + chain(STATE_CHUNKS)
        + [block(STATE_CHUNKS)]
        + chain(STATE_CHUNKS)
        + chain(GROUPS)
        + [
            block(PLANE),
            block(line),
            pltpu.SemaphoreType.DMA((5,)),
            pltpu.SemaphoreType.DMA((2,)),
            pltpu.SemaphoreType.DMA((2,)),
            pltpu.SemaphoreType.DMA((14,)),
            pltpu.SemaphoreType.DMA((14,)),
            pltpu.SemaphoreType.REGULAR,
        ],
        compiler_params=pltpu.CompilerParams(
            collective_id=0, has_side_effects=True, vmem_limit_bytes=32 * 1024 * 1024
        ),
    )(q, k, v, g, w)

    gq, gk, gv, gw = pl.pallas_call(
        finish_kernel,
        out_shape=(
            jax.ShapeDtypeStruct(flat, BF16),
            jax.ShapeDtypeStruct(flat, BF16),
            jax.ShapeDtypeStruct(flat, BF16),
            jax.ShapeDtypeStruct((3, 3, CHANNELS), F32),
        ),
        in_specs=[vmem] * 6,
        out_specs=(hbm,) * 4,
        scratch_shapes=[
            pltpu.VMEM(flat, BF16),
            pltpu.SemaphoreType.DMA((3,)),
            pltpu.SemaphoreType.DMA((1,)),
        ],
        compiler_params=pltpu.CompilerParams(vmem_limit_bytes=32 * 1024 * 1024),
    )(gq, gv, dk, gw, kb, gks)
    return gq.reshape(shape), gk.reshape(shape), gv.reshape(shape), gw


def solution(mesh):
    sizes = (mesh.shape["tm"], mesh.shape["rows"])
    placed = P("tm", "rows", None, None)
    return jax.shard_map(
        functools.partial(shards, sizes),
        mesh=mesh,
        in_specs=(placed, placed, placed, placed, P()),
        out_specs=(placed, placed, placed, P()),
        check_vma=False,
    )
```
